256 devices in a mesh: row: 8 (over z), rep: 32 (over x, y, core).
Axes of the slice: x: 4, y: 4, z: 8, core: 2. Of those that a mesh axis runs over, the one named last changes fastest.
Arguments:
- feats: bfloat16 [131072, 128], P(('row', 'rep')), may hold values from -6 to 6
- w_self: bfloat16 [128, 256], replicated, may hold values from -0.5 to 0.5
- w_neigh: bfloat16 [128, 256], replicated, may hold values from -0.5 to 0.5
- bias: float32 [256], replicated, may hold values from -3 to 3
- tiles: bfloat16 [8, 32, 256, 128, 128], P('row', 'rep'), may hold values from 0 to 0.2
- tile_row: int32 [8, 32, 256], P('row', 'rep'), may hold values from 0 to 127
- tile_col: int32 [8, 32, 256], P('row', 'rep'), may hold values from 0 to 31
- tile_count: int32 [8, 32], P('row', 'rep'), may hold values from 64 to 256, as said below
- cotangent: bfloat16 [131072, 256], P(('row', 'rep')), may hold values from -6 to 6
Outputs:
- out: bfloat16 [131072, 256], P(('row', 'rep'))
- grad_feats: float32 [131072, 128], P(('row', 'rep'))
- grad_w_self: float32 [128, 256], replicated
- grad_w_neigh: float32 [128, 256], replicated
- grad_bias: float32 [256], replicated
The draws below stay inside these ranges and needn't reach their ends.
Inputs may be any that keep to these rules, and one draw needn't show every extreme that they name: Tiles at or past tile_count of their device are ignored; on some device all 256 tiles are live.
All inputs are finite; a program needn't handle non-finite values.
Results may differ from the reference program's by a relative error of at most 0.025.
Values may be sent and summed in bfloat16 or wider, within the bound.
No kernel may reach another device: no remote copies, remote signals or barrier semaphores. Data moves between devices by JAX's collectives and lax.ppermute only.
A program may use at most 128 MiB of HBM per device.

```python
import jax
import jax.numpy as jnp
from jax import lax

F = 128
H = 256
TILE = 128
ROWS_DEV = 512
BLK_DEV = 256
NODES = 131072
SLAB_BLK = 128
SECTION_BLK = 32
N_ROW = 8
N_REP = 32


def draw_tile_count(key, part):
    key = jax.random.fold_in(key, 7)
    first_key, second_key = jax.random.split(key)
    total = N_ROW * N_REP
    counts = jax.random.randint(first_key, (total,), max(BLK_DEV // 4, 1), BLK_DEV + 1, dtype=jnp.int32)
    busiest = jax.random.randint(second_key, (), 0, total, dtype=jnp.int32)
    counts = jnp.where(jnp.arange(total, dtype=jnp.int32) == busiest, BLK_DEV, counts)
    return counts.reshape(N_ROW, N_REP).astype(jnp.int32)


def draw_tiles(key, part):
    key = jax.random.fold_in(key, 11)
    mask_key, value_key = jax.random.split(key)
    shape = (N_ROW, N_REP, BLK_DEV, TILE, TILE)
    present = jax.random.uniform(mask_key, shape, jnp.float32) < 0.125
    values = jnp.exp(jax.random.uniform(value_key, shape, jnp.float32, jnp.log(0.02), jnp.log(0.19)))
    return jnp.where(present, values, 0.0).astype(jnp.bfloat16)


def touch_ends(entries, own_key, low, top_value):
    shape = entries.shape
    spot = [jax.random.randint(jax.random.fold_in(own_key, axis), (), 0, shape[axis]) for axis in range(len(shape))]
    entries = entries.at[tuple(spot)].set(low)
    longest = shape.index(max(shape))
    spot[longest] = (spot[longest] + 1) % shape[longest]
    return entries.at[tuple(spot)].set(top_value)


def block_levels(own_key, dims, cuts, least, high):
    loudness, own = 1.0, jax.random.fold_in(own_key, 6)
    for dim, shards_of in cuts:
        steps = jnp.exp(jax.random.uniform(jax.random.fold_in(own, dim), (shards_of,), jnp.float32, least / len(cuts), high / len(cuts)))
        loudness = loudness * jnp.repeat(steps, dims[dim] // shards_of).reshape([-1 if axis == dim else 1 for axis in range(len(dims))])
    return loudness


def bell_draw(stream_key, extent, deviation, reach, pieces=(), kind=jnp.bfloat16):
    drawn = jax.random.normal(stream_key, extent, jnp.float32) * deviation
    if len(pieces) > 0:
        drawn = block_levels(stream_key, extent, pieces, -0.22, 0.18) * drawn
    return jnp.clip(drawn, min=-reach, max=reach).astype(kind)


def setup_inputs(seed: int = 0) -> dict:
    key_of = jax.random.split(jax.random.key(seed), 10)
    return {
        "feats": bell_draw(key_of[0], (NODES, F), 1.0, 6.0, ((0, 256),)),
        "w_self": bell_draw(key_of[1], (F, H), F ** -0.5, 0.5),
        "w_neigh": bell_draw(key_of[2], (F, H), F ** -0.5, 0.5),
        "bias": bell_draw(key_of[3], (H,), 0.5, 3.0, (), jnp.float32),
        "tiles": draw_tiles(jax.random.fold_in(key_of[9], 71), 0),
        "tile_row": touch_ends(jax.random.randint(key_of[5], (N_ROW, N_REP, BLK_DEV), 0, ROWS_DEV * N_REP // TILE), jax.random.fold_in(key_of[5], 1), 0, (ROWS_DEV * N_REP // TILE) - 1).astype(jnp.int32),
        "tile_col": touch_ends(jax.random.randint(key_of[6], (N_ROW, N_REP, BLK_DEV), 0, ROWS_DEV * N_ROW // TILE), jax.random.fold_in(key_of[6], 1), 0, (ROWS_DEV * N_ROW // TILE) - 1).astype(jnp.int32),
        "tile_count": draw_tile_count(jax.random.fold_in(key_of[9], 71), 0),
        "cotangent": bell_draw(key_of[8], (NODES, H), 1.0, 6.0, ((0, 256),)),
    }


def reference(feats, w_self, w_neigh, bias, tiles, tile_row, tile_col, tile_count, cotangent):
    devices_all = N_ROW * N_REP
    slab_rows = ROWS_DEV * N_REP
    section_rows = ROWS_DEV * N_ROW
    grid_feats = feats.reshape(N_ROW, N_REP, ROWS_DEV, F)
    flat_tiles = tiles.reshape(devices_all, BLK_DEV, TILE, TILE)
    flat_rows = tile_row.reshape(devices_all, BLK_DEV)
    flat_cols = tile_col.reshape(devices_all, BLK_DEV)
    flat_count = tile_count.reshape(devices_all)
    slot_index = jnp.arange(BLK_DEV, dtype=jnp.int32)

    def forward_step(carry, index):
        r_index = index // N_REP
        p_index = index % N_REP
        section_blocks = lax.dynamic_index_in_dim(grid_feats, p_index, 1, keepdims=False).reshape(SECTION_BLK, TILE, F)
        picked = section_blocks[flat_cols[index]]
        live = (slot_index < flat_count[index]).astype(jnp.float32)
        prods = jnp.einsum('bij,bjf->bif', flat_tiles[index].astype(jnp.float32), picked.astype(jnp.float32))
        place = (flat_rows[index][None, :] == jnp.arange(SLAB_BLK, dtype=jnp.int32)[:, None]).astype(jnp.float32) * live[None, :]
        partial_value = jnp.einsum('qb,bif->qif', place, prods).reshape(slab_rows, F)
        return (carry.at[r_index].add(partial_value), None)
    agg_sum, _ = lax.scan(forward_step, jnp.zeros((N_ROW, slab_rows, F), jnp.float32), jnp.arange(devices_all, dtype=jnp.int32))
    agg = agg_sum.reshape(NODES, F).astype(jnp.bfloat16)
    z = jnp.dot(feats, w_self, preferred_element_type=jnp.float32) + jnp.dot(agg, w_neigh, preferred_element_type=jnp.float32) + bias
    out, backward = jax.vjp(jax.nn.gelu, z)
    dz = backward(cotangent.astype(jnp.float32))[0].astype(jnp.bfloat16)
    rescale = 1.0 / jnp.sqrt(jnp.float32(NODES))
    grad_w_self = jnp.dot(feats.T, dz, preferred_element_type=jnp.float32) * rescale
    grad_w_neigh = jnp.dot(agg.T, dz, preferred_element_type=jnp.float32) * rescale
    grad_bias = lax.optimization_barrier(jnp.sum(dz.astype(jnp.float32), axis=0)) * rescale
    dzn = jnp.dot(dz, w_neigh.T, preferred_element_type=jnp.float32).astype(jnp.bfloat16)
    slab_dzn = dzn.reshape(N_ROW, SLAB_BLK, TILE, F)

    def backward_step(carry, index):
        r_index = index // N_REP
        p_index = index % N_REP
        slab_blocks = lax.dynamic_index_in_dim(slab_dzn, r_index, 0, keepdims=False)
        picked = slab_blocks[flat_rows[index]]
        live = (slot_index < flat_count[index]).astype(jnp.float32)
        trans = jnp.einsum('bij,bif->bjf', flat_tiles[index].astype(jnp.float32), picked.astype(jnp.float32))
        place = (flat_cols[index][None, :] == jnp.arange(SECTION_BLK, dtype=jnp.int32)[:, None]).astype(jnp.float32) * live[None, :]
        partial_value = jnp.einsum('cb,bjf->cjf', place, trans).reshape(N_ROW, ROWS_DEV, F)
        return (carry.at[:, p_index].add(partial_value), None)
    spread, _ = lax.scan(backward_step, jnp.zeros((N_ROW, N_REP, ROWS_DEV, F), jnp.float32), jnp.arange(devices_all, dtype=jnp.int32))
    grad_feats = jnp.dot(dz, w_self.T, preferred_element_type=jnp.float32) + spread.reshape(NODES, F)
    return (out.astype(jnp.bfloat16), grad_feats, grad_w_self, grad_w_neigh, grad_bias)
```

```python
import jax
import jax.numpy as jnp
from jax import lax
from jax.experimental import pallas as pl
from jax.experimental.pallas import tpu as pltpu
from jax.sharding import PartitionSpec as P

T = 128
SLOTS = 256
CHUNK = 8
GROUP = 4
BF = jnp.bfloat16
F32 = jnp.float32
VMEM_LIMIT = 48 * 1024 * 1024

VM = pl.BlockSpec(memory_space=pltpu.VMEM)
SM = pl.BlockSpec(memory_space=pltpu.SMEM)
HB = pl.BlockSpec(memory_space=pl.ANY)


def shape(rows, cols, dtype):
    return jax.ShapeDtypeStruct((rows, cols), dtype)


def rep_move(value, dx, dy, dc):
    pairs = [
        ((x * 4 + y) * 2 + c, ((x ^ dx) * 4 + (y ^ dy)) * 2 + (c ^ dc))
        for x in range(4)
        for y in range(4)
        for c in range(2)
    ]
    return lax.ppermute(value, "rep", pairs)


def row_move(value, step):
    return lax.ppermute(value, "row", [(i, (i + step) % 8) for i in range(8)])


def row_swap(value, bit):
    return lax.ppermute(value, "row", [(i, i ^ bit) for i in range(8)])


def tile_copy(tiles, tbuf, sem, i):
    part = pl.ds(pl.multiple_of(i * CHUNK, CHUNK), CHUNK)
    return pltpu.make_async_copy(tiles.at[part], tbuf.at[part], sem.at[i])


def start_tiles(count, tiles, tbuf, sem):
    chunks = (count[0] + CHUNK - 1) // CHUNK

    def start(i, carry):
        tile_copy(tiles, tbuf, sem, i).start()
        return carry

    lax.fori_loop(0, chunks, start, 0)
    return chunks


def zero(acc):
    def clear(i, carry):
        acc[i] = jnp.zeros((T, T), F32)
        return carry

    lax.fori_loop(0, acc.shape[0], clear, 0, unroll=4)


def add_products(chunks, tiles, tbuf, sem, product, place, acc):
    def step(i, carry):
        tile_copy(tiles, tbuf, sem, i).wait()
        for g in range(0, CHUNK, GROUP):
            slots = [i * CHUNK + g + k for k in range(GROUP)]
            prods = [product(t) for t in slots]
            for t, prod in zip(slots, prods):
                q = place[t]
                acc[q] = acc[q] + prod
        return carry

    lax.fori_loop(0, chunks, step, 0)


def forward_kernel(count, place, source, tiles, *rest):
    feats, outs = rest[:9], rest[9:25]
    tbuf, fbuf, acc, stage, tsem, fsem, osem = rest[25:]
    loads = []
    for d in range(8):
        if d == 4:
            loads.append(pltpu.make_async_copy(feats[4], fbuf.at[pl.ds(16, 2)], fsem.at[4]))
            loads.append(pltpu.make_async_copy(feats[8], fbuf.at[pl.ds(18, 2)], fsem.at[8]))
        else:
            loads.append(pltpu.make_async_copy(feats[d], fbuf.at[pl.ds(4 * d, 4)], fsem.at[d]))
    for load in loads:
        load.start()
    chunks = start_tiles(count, tiles, tbuf, tsem)
    zero(acc)
    for load in loads:
        load.wait()

    def product(t):
        return jnp.dot(tbuf[t], fbuf[source[t]], preferred_element_type=F32)

    add_products(chunks, tiles, tbuf, tsem, product, place, acc)
    stores = []
    for k in range(8):
        part = pl.ds(8 * k, 8)
        stage[part] = acc[part].astype(BF)
        stores.append(pltpu.make_async_copy(stage.at[part], outs[k], osem.at[k]))
        stores[-1].start()
    for k in range(8):
        stores.append(pltpu.make_async_copy(acc.at[pl.ds(64 + 8 * k, 8)], outs[8 + k], osem.at[8 + k]))
        stores[-1].start()
    for store in stores:
        store.wait()


def forward(count, place, source, tiles, feats):
    blocks = [jax.ShapeDtypeStruct((8, T, T), BF)] * 8 + [jax.ShapeDtypeStruct((8, T, T), F32)] * 8
    return pl.pallas_call(
        forward_kernel,
        out_shape=blocks,
        in_specs=[SM, SM, SM, HB] + [HB] * 9,
        out_specs=[HB] * 16,
        scratch_shapes=[
            pltpu.VMEM((SLOTS, T, T), BF),
            pltpu.VMEM((32, T, T), BF),
            pltpu.VMEM((129, T, T), F32),
            pltpu.VMEM((64, T, T), BF),
            pltpu.SemaphoreType.DMA((SLOTS // CHUNK,)),
            pltpu.SemaphoreType.DMA((9,)),
            pltpu.SemaphoreType.DMA((16,)),
        ],
        compiler_params=pltpu.CompilerParams(vmem_limit_bytes=VMEM_LIMIT),
        cost_estimate=pl.CostEstimate(flops=2 * SLOTS * T**3, bytes_accessed=16 * 2**20, transcendentals=0),
        name="tiles_forward",
    )(count, place, source, tiles, *feats)


def backward_kernel(count, place, source, tiles, *rest):
    grads, outs = rest[:16], rest[16:25]
    tbuf, gbuf, acc, stage, tsem, gsem, osem = rest[25:]
    loads = [
        pltpu.make_async_copy(grads[k].at[pl.ds(0, 8 * T)], gbuf.at[pl.ds(8 * T * k, 8 * T)], gsem.at[k])
        for k in range(16)
    ]
    for load in loads:
        load.start()
    chunks = start_tiles(count, tiles, tbuf, tsem)
    zero(acc)
    for load in loads:
        load.wait()

    def product(t):
        grad = gbuf[pl.ds(pl.multiple_of(source[t] * T, T), T)]
        return jnp.dot(grad, tbuf[t], preferred_element_type=F32)

    add_products(chunks, tiles, tbuf, tsem, product, place, acc)
    stores = [pltpu.make_async_copy(acc.at[pl.ds(0, 4)], outs[0], osem.at[0])]
    stores[0].start()
    for d in range(1, 8):
        stage[pl.ds(4 * d, 4)] = acc[pl.ds(4 * d, 4)].astype(BF)
        if d == 4:
            stores.append(pltpu.make_async_copy(stage.at[pl.ds(16, 2)], outs[4], osem.at[4]))
            stores.append(pltpu.make_async_copy(stage.at[pl.ds(18, 2)], outs[8], osem.at[8]))
            stores[-2].start()
        else:
            stores.append(pltpu.make_async_copy(stage.at[pl.ds(4 * d, 4)], outs[d], osem.at[d]))
        stores[-1].start()
    for store in stores:
        store.wait()


def backward(count, place, source, tiles, grads):
    four = jax.ShapeDtypeStruct((4, T, T), BF)
    two = jax.ShapeDtypeStruct((2, T, T), BF)
    outs = [jax.ShapeDtypeStruct((4, T, T), F32), four, four, four, two, four, four, four, two]
    return pl.pallas_call(
        backward_kernel,
        out_shape=outs,
        in_specs=[SM, SM, SM, HB] + [HB] * 16,
        out_specs=[HB] * 9,
        scratch_shapes=[
            pltpu.VMEM((SLOTS, T, T), BF),
            pltpu.VMEM((128 * T, T), BF),
            pltpu.VMEM((33, T, T), F32),
            pltpu.VMEM((32, T, T), BF),
            pltpu.SemaphoreType.DMA((SLOTS // CHUNK,)),
            pltpu.SemaphoreType.DMA((16,)),
            pltpu.SemaphoreType.DMA((9,)),
        ],
        compiler_params=pltpu.CompilerParams(vmem_limit_bytes=VMEM_LIMIT),
        cost_estimate=pl.CostEstimate(flops=2 * SLOTS * T**3, bytes_accessed=16 * 2**20, transcendentals=0),
        name="tiles_backward",
    )(count, place, source, tiles, *grads)


def layer_kernel(
    my_y, a0, a1, a2, a3, b0, b1, b2, b3, feats, w_self, w_neigh, bias, cot,
    out, base, da, db, pay1, pay2, pay3, own_w, gbuf,
):
    agg_a = (a0[...].astype(F32) + a1[...].astype(F32)) + (a2[...].astype(F32) + a3[...].astype(F32))
    agg_b = (b0[...].astype(F32) + b1[...].astype(F32)) + (b2[...].astype(F32) + b3[...].astype(F32))
    agg = jnp.concatenate([agg_a, agg_b], axis=0).astype(BF)
    x = feats[...]
    z = (
        jnp.dot(x, w_self[...], preferred_element_type=F32)
        + jnp.dot(agg, w_neigh[...], preferred_element_type=F32)
        + bias[...]
    )
    root = 0.7978845608028654
    t = jnp.tanh(root * (z + 0.044715 * (z * z * z)))
    cdf = 0.5 * (1.0 + t)
    out[...] = (z * cdf).astype(BF)
    slope = cdf + 0.5 * z * (1.0 - t * t) * (root * (1.0 + 3.0 * 0.044715 * (z * z)))
    dz = (cot[...].astype(F32) * slope).astype(BF)
    turned = lax.dot_general(w_neigh[...], dz, (((1,), (1,)), ((), ())), preferred_element_type=F32).astype(BF)
    for s in range(2):
        da[s] = turned[:, T * s : T * s + T]
        db[s] = turned[:, T * (2 + s) : T * (3 + s)]
    both = jnp.concatenate([x, agg], axis=1)
    grads = lax.dot_general(both, dz, (((0,), (0,)), ((), ())), preferred_element_type=F32)
    column = jnp.sum(dz.astype(F32), axis=0, keepdims=True)
    for y in range(4):
        gbuf[y, 0:64] = grads[64 * y : 64 * y + 64, 0:T].astype(BF)
        gbuf[y, 64:128] = grads[64 * y : 64 * y + 64, T : 2 * T].astype(BF)
    columns = jnp.concatenate([column[:, 0:T], column[:, T : 2 * T]], axis=0)
    high = columns.astype(BF)
    low = (columns - high.astype(F32)).astype(BF)
    tail = jnp.concatenate([high.astype(F32), low.astype(F32), jnp.zeros((12, T), F32)], axis=0).astype(BF)
    for k, pay in ((0, own_w), (1, pay1), (2, pay2), (3, pay3)):
        offset = 0
        if k:
            for s in range(2):
                pay[T * s : T * s + T] = da[s]
            offset = 2 * T
        pay[offset : offset + T] = gbuf[my_y[0] ^ k]
        pay[offset + T : offset + T + 16] = tail
    base[...] = lax.dot_general(dz, w_self[...], (((1,), (1,)), ((), ())), preferred_element_type=F32)


def layer(my_y, parts_a, parts_b, feats, w_self, w_neigh, bias, cot):
    rows = feats.shape[0]
    pair = jax.ShapeDtypeStruct((2, T, T), BF)
    pay = shape(2 * T + T + 16, T, BF)
    return pl.pallas_call(
        layer_kernel,
        out_shape=[shape(rows, 2 * T, BF), shape(rows, T, F32), pair, pair, pay, pay, pay, shape(T + 16, T, BF)],
        in_specs=[SM] + [VM] * 13,
        out_specs=[VM] * 8,
        scratch_shapes=[pltpu.VMEM((4, T, T), BF)],
        compiler_params=pltpu.CompilerParams(vmem_limit_bytes=VMEM_LIMIT),
        name="layer",
    )(my_y, *parts_a, *parts_b, feats, w_self, w_neigh, bias, cot)


def weights_kernel(my_y, scale, c0, c1, c2, c3, g_self, g_neigh, g_bias, whole):
    for k, c in enumerate((c0, c1, c2, c3)):
        at = pl.ds(pl.multiple_of((my_y[0] ^ k) * 64, 64), 64)
        whole[at, 0:T] = c[0:64] * scale[0]
        whole[at, T : 2 * T] = c[64:128] * scale[0]
    g_self[...] = whole[0:T]
    g_neigh[...] = whole[T : 2 * T]
    g_bias[...] = (c0[T : T + 2] + c0[T + 2 : T + 4]) * scale[0]


def weights(my_y, scale, chunks):
    return pl.pallas_call(
        weights_kernel,
        out_shape=[shape(T, 2 * T, F32), shape(T, 2 * T, F32), shape(2, T, F32)],
        in_specs=[SM, SM] + [VM] * 4,
        out_specs=[VM] * 3,
        scratch_shapes=[pltpu.VMEM((2 * T, 2 * T), F32)],
        name="weights",
    )(my_y, scale, *chunks)


def finish_kernel(base, p0, f1, b1, f2, b2, grad):
    for s in range(4):
        spread = (
            p0[s] + (f1[s].astype(F32) + b1[s].astype(F32)) + (f2[s].astype(F32) + b2[s].astype(F32))
        )
        grad[T * s : T * s + T] = base[T * s : T * s + T] + spread.T


def finish(base, p0, f1, b1, f2, b2):
    return pl.pallas_call(
        finish_kernel,
        out_shape=shape(base.shape[0], T, F32),
        in_specs=[VM] * 6,
        out_specs=VM,
        name="finish",
    )(base, p0, f1, b1, f2, b2)


def wide_sum(values):
    values = [value.astype(F32) for value in values]
    return (values[0] + values[1]) + (values[2] + values[3])


def per_device(feats, w_self, w_neigh, bias, tiles, tile_row, tile_col, tile_count, cotangent):
    rows_dev, width = feats.shape
    total_nodes = rows_dev * 256
    tiles = tiles.reshape(SLOTS, T, T)
    my_z = lax.axis_index("row")
    my_rep = lax.axis_index("rep")
    my_x, my_y, my_c = my_rep // 8, (my_rep // 2) % 4, my_rep % 2
    y_arg = my_y.reshape(1)
    count = tile_count.reshape(1)
    live = jnp.arange(SLOTS, dtype=jnp.int32) < count
    row = tile_row.reshape(SLOTS)
    col = tile_col.reshape(SLOTS)

    owner, sub = row // 4, row % 4
    kx, ky, kc = (owner // 8) ^ my_x, ((owner // 2) % 4) ^ my_y, (owner % 2) ^ my_c
    in_half = jnp.where(sub < 2, (kx * 4 + ky) * 2 + sub, 32 + (ky * 4 + kx) * 2 + sub - 2)
    slab_place = jnp.where(live, in_half + 64 * (1 - kc), 128)
    slab_source = in_half + 64 * kc
    col_block = ((col // 4 - my_z) % 8) * 4 + col % 4
    section_place = jnp.where(live, col_block, 32)

    blocks = [feats] + [None] * 8
    up = down = feats
    for step in range(1, 4):
        up, down = row_move(up, 1), row_move(down, -1)
        blocks[8 - step], blocks[step] = up, down
    blocks[4] = row_move(up[: rows_dev // 2], 1)
    blocks[8] = row_move(down[rows_dev // 2 :], -1)
    blocks = [block.reshape(-1, T, T) for block in blocks]

    parts = forward(count, slab_place, col_block, tiles, blocks)
    order = (2, 6, 1, 5, 3, 7, 0, 4)
    both = [None] * 8
    for k in order:
        got = rep_move(parts[k], 0, 0, 1)
        both[k] = parts[8 + k] + got.astype(F32)
    part_a, part_b = [both[0]], [both[4]]
    got_a, got_b = {}, {}
    for k in (2, 1, 3):
        got_a[k] = rep_move(both[k].astype(BF), k, 0, 0)
        got_b[k] = rep_move(both[4 + k].astype(BF), 0, k, 0)
    sum_a = wide_sum([both[0], got_a[1], got_a[2], got_a[3]])
    sum_b = wide_sum([both[4], got_b[1], got_b[2], got_b[3]])
    last_a, last_b = [sum_a[0:2]], [sum_b[0:2]]
    for k in (1, 2, 3):
        last_a.append(rep_move(sum_a[2 * k : 2 * k + 2].astype(BF), 0, k, 0))
        last_b.append(rep_move(sum_b[2 * k : 2 * k + 2].astype(BF), k, 0, 0))
    last_a = [v.reshape(2 * T, T) for v in last_a]
    last_b = [v.reshape(2 * T, T) for v in last_b]

    out, base, da, db, pay1, pay2, pay3, own_w = layer(
        y_arg, last_a, last_b, feats, w_self, w_neigh, bias.reshape(1, -1), cotangent
    )

    got_a, got_b = {}, {}
    for k, pay in ((2, pay2), (1, pay1), (3, pay3)):
        got_a[k] = rep_move(pay, 0, k, 0)
        got_b[k] = rep_move(db, k, 0, 0)
    gw = wide_sum([own_w] + [got_a[k][2 * T :] for k in (1, 2, 3)]).astype(BF)
    bundle_a = jnp.concatenate([da.reshape(2 * T, T)] + [got_a[k][: 2 * T] for k in (1, 2, 3)] + [gw], axis=0)
    bundle_b = jnp.concatenate([db] + [got_b[k] for k in (1, 2, 3)], axis=0).reshape(8 * T, T)
    all_a, all_b = [bundle_a, None, None, None], [bundle_b, None, None, None]
    for k in (2, 1, 3):
        all_a[k] = rep_move(bundle_a, k, 0, 0)
        all_b[k] = rep_move(bundle_b, 0, k, 0)
    own = all_a + all_b
    grads = own + [rep_move(v, 0, 0, 1) for v in own]

    p = backward(count, section_place, slab_source, tiles, grads)
    up3, down3 = row_move(p[3], 1), row_move(p[5], -1)
    up4, down4 = row_move(p[4], 2), row_move(p[8], -2)
    up1, down1 = row_move(p[1], 1), row_move(p[7], -1)
    zeros = jnp.zeros((2, T, T), F32)
    up2 = p[2].astype(F32) + up3.astype(F32) + jnp.concatenate([up4.astype(F32), zeros], axis=0)
    down2 = p[6].astype(F32) + down3.astype(F32) + jnp.concatenate([zeros, down4.astype(F32)], axis=0)
    up2, down2 = row_move(up2.astype(BF), 2), row_move(down2.astype(BF), -2)
    grad_feats = finish(base, p[0], up1, down1, up2, down2)

    gw = wide_sum([v[8 * T :] for v in all_a]).astype(BF)
    gw = gw.astype(F32) + rep_move(gw, 0, 0, 1).astype(F32)
    for bit in (1, 2, 4):
        gw = gw.astype(BF)
        gw = gw.astype(F32) + row_swap(gw, bit).astype(F32)
    quarters = [gw] + [rep_move(gw, 0, k, 0) for k in (1, 2, 3)]
    scale = (1.0 / jnp.sqrt(jnp.float32(total_nodes))).reshape(1)
    grad_self, grad_neigh, grad_bias = weights(y_arg, scale, quarters)
    return out, grad_feats, grad_self, grad_neigh, grad_bias.reshape(-1)


def solution(mesh):
    placed = (
        P(("row", "rep"), None),
        P(),
        P(),
        P(),
        P("row", "rep", None, None, None),
        P("row", "rep", None),
        P("row", "rep", None),
        P("row", "rep"),
        P(("row", "rep"), None),
    )
    return jax.shard_map(
        per_device,
        mesh=mesh,
        in_specs=placed,
        out_specs=(P(("row", "rep"), None), P(("row", "rep"), None), P(), P(), P()),
        check_vma=False,
    )
```

```python
import jax
import jax.numpy as jnp
from jax import lax
from jax.experimental import pallas as pl
from jax.experimental.pallas import tpu as pltpu
from jax.sharding import PartitionSpec as P

T = 128
SLOTS = 256
CHUNK = 8
GROUP = 4
BF = jnp.bfloat16
F32 = jnp.float32
VMEM_LIMIT = 48 * 1024 * 1024

VM = pl.BlockSpec(memory_space=pltpu.VMEM)
SM = pl.BlockSpec(memory_space=pltpu.SMEM)
HB = pl.BlockSpec(memory_space=pl.ANY)


def shape(rows, cols, dtype):
    return jax.ShapeDtypeStruct((rows, cols), dtype)


def other_core(value):
    return lax.ppermute(value, "rep", [(i, i ^ 1) for i in range(32)])


def axis_move(value, which, k):
    return lax.ppermute(value, "rep", [(i, i ^ (k * (8 if i % 2 == which else 2))) for i in range(32)])


def row_move(value, step):
    return lax.ppermute(value, "row", [(i, (i + step) % 8) for i in range(8)])


def row_swap(value, bit):
    return lax.ppermute(value, "row", [(i, i ^ bit) for i in range(8)])


def tile_copy(tiles, tbuf, sem, i):
    part = pl.ds(pl.multiple_of(i * CHUNK, CHUNK), CHUNK)
    return pltpu.make_async_copy(tiles.at[part], tbuf.at[part], sem.at[i])


def start_tiles(count, tiles, tbuf, sem):
    chunks = (count[0] + CHUNK - 1) // CHUNK

    def start(i, carry):
        tile_copy(tiles, tbuf, sem, i).start()
        return carry

    lax.fori_loop(0, chunks, start, 0)
    return chunks


def zero(acc):
    def clear(i, carry):
        acc[i] = jnp.zeros((T, T), F32)
        return carry

    lax.fori_loop(0, acc.shape[0], clear, 0, unroll=4)


def add_products(chunks, tiles, tbuf, sem, product, place, acc):
    def step(i, carry):
        tile_copy(tiles, tbuf, sem, i).wait()
        for g in range(0, CHUNK, GROUP):
            slots = [i * CHUNK + g + k for k in range(GROUP)]
            prods = [product(t) for t in slots]
            for t, prod in zip(slots, prods):
                q = place[t]
                acc[q] = acc[q] + prod
        return carry

    lax.fori_loop(0, chunks, step, 0)


def forward_kernel(count, place, source, tiles, *rest):
    feats, outs = rest[:9], rest[9:17]
    tbuf, fbuf, acc, stage, tsem, fsem, osem = rest[17:]
    loads = []
    for d in range(8):
        if d == 4:
            loads.append(pltpu.make_async_copy(feats[4], fbuf.at[pl.ds(16, 2)], fsem.at[4]))
            loads.append(pltpu.make_async_copy(feats[8], fbuf.at[pl.ds(18, 2)], fsem.at[8]))
        else:
            loads.append(pltpu.make_async_copy(feats[d], fbuf.at[pl.ds(4 * d, 4)], fsem.at[d]))
    for load in loads:
        load.start()
    chunks = start_tiles(count, tiles, tbuf, tsem)
    zero(acc)
    for load in loads:
        load.wait()

    def product(t):
        return jnp.dot(tbuf[t], fbuf[source[t]], preferred_element_type=F32)

    add_products(chunks, tiles, tbuf, tsem, product, place, acc)
    stores = []
    for k in range(8):
        part = pl.ds(16 * k, 16)
        stage[part] = acc[part].astype(BF)
        stores.append(pltpu.make_async_copy(stage.at[part], outs[k], osem.at[k]))
        stores[-1].start()
    for store in stores:
        store.wait()


def forward(count, place, source, tiles, feats):
    blocks = [jax.ShapeDtypeStruct((16, T, T), BF)] * 8
    return pl.pallas_call(
        forward_kernel,
        out_shape=blocks,
        in_specs=[SM, SM, SM, HB] + [HB] * 9,
        out_specs=[HB] * 8,
        scratch_shapes=[
            pltpu.VMEM((SLOTS, T, T), BF),
            pltpu.VMEM((32, T, T), BF),
            pltpu.VMEM((129, T, T), F32),
            pltpu.VMEM((128, T, T), BF),
            pltpu.SemaphoreType.DMA((SLOTS // CHUNK,)),
            pltpu.SemaphoreType.DMA((9,)),
            pltpu.SemaphoreType.DMA((8,)),
        ],
        compiler_params=pltpu.CompilerParams(vmem_limit_bytes=VMEM_LIMIT),
        cost_estimate=pl.CostEstimate(flops=2 * SLOTS * T**3, bytes_accessed=16 * 2**20, transcendentals=0),
        name="tiles_forward",
    )(count, place, source, tiles, *feats)


def backward_kernel(count, place, source, tiles, *rest):
    grads, outs = rest[:8], rest[8:17]
    tbuf, gbuf, acc, stage, tsem, gsem, osem = rest[17:]
    loads = [
        pltpu.make_async_copy(grads[k].at[pl.ds(0, 16 * T)], gbuf.at[pl.ds(16 * T * k, 16 * T)], gsem.at[k])
        for k in range(8)
    ]
    for load in loads:
        load.start()
    chunks = start_tiles(count, tiles, tbuf, tsem)
    zero(acc)
    for load in loads:
        load.wait()

    def product(t):
        grad = gbuf[pl.ds(pl.multiple_of(source[t] * T, T), T)]
        return jnp.dot(grad, tbuf[t], preferred_element_type=F32)

    add_products(chunks, tiles, tbuf, tsem, product, place, acc)
    stores = [pltpu.make_async_copy(acc.at[pl.ds(0, 4)], outs[0], osem.at[0])]
    stores[0].start()
    for d in range(1, 8):
        stage[pl.ds(4 * d, 4)] = acc[pl.ds(4 * d, 4)].astype(BF)
        if d == 4:
            stores.append(pltpu.make_async_copy(stage.at[pl.ds(16, 2)], outs[4], osem.at[4]))
            stores.append(pltpu.make_async_copy(stage.at[pl.ds(18, 2)], outs[8], osem.at[8]))
            stores[-2].start()
        else:
            stores.append(pltpu.make_async_copy(stage.at[pl.ds(4 * d, 4)], outs[d], osem.at[d]))
        stores[-1].start()
    for store in stores:
        store.wait()


def backward(count, place, source, tiles, grads):
    four = jax.ShapeDtypeStruct((4, T, T), BF)
    two = jax.ShapeDtypeStruct((2, T, T), BF)
    outs = [jax.ShapeDtypeStruct((4, T, T), F32), four, four, four, two, four, four, four, two]
    return pl.pallas_call(
        backward_kernel,
        out_shape=outs,
        in_specs=[SM, SM, SM, HB] + [HB] * 8,
        out_specs=[HB] * 9,
        scratch_shapes=[
            pltpu.VMEM((SLOTS, T, T), BF),
            pltpu.VMEM((128 * T, T), BF),
            pltpu.VMEM((33, T, T), F32),
            pltpu.VMEM((32, T, T), BF),
            pltpu.SemaphoreType.DMA((SLOTS // CHUNK,)),
            pltpu.SemaphoreType.DMA((8,)),
            pltpu.SemaphoreType.DMA((9,)),
        ],
        compiler_params=pltpu.CompilerParams(vmem_limit_bytes=VMEM_LIMIT),
        cost_estimate=pl.CostEstimate(flops=2 * SLOTS * T**3, bytes_accessed=16 * 2**20, transcendentals=0),
        name="tiles_backward",
    )(count, place, source, tiles, *grads)


def layer_kernel(
    my_first, a0, a1, a2, a3, feats, w_self, w_neigh, bias, cot,
    out, base, dzn, pay1, pay2, pay3, own_w, gbuf,
):
    agg = (a0[...] + a1[...].astype(F32)) + (a2[...].astype(F32) + a3[...].astype(F32))
    agg = agg.astype(BF)
    x = feats[...]
    z = (
        jnp.dot(x, w_self[...], preferred_element_type=F32)
        + jnp.dot(agg, w_neigh[...], preferred_element_type=F32)
        + bias[...]
    )
    root = 0.7978845608028654
    t = jnp.tanh(root * (z + 0.044715 * (z * z * z)))
    cdf = 0.5 * (1.0 + t)
    out[...] = (z * cdf).astype(BF)
    slope = cdf + 0.5 * z * (1.0 - t * t) * (root * (1.0 + 3.0 * 0.044715 * (z * z)))
    dz = (cot[...].astype(F32) * slope).astype(BF)
    turned = lax.dot_general(w_neigh[...], dz, (((1,), (1,)), ((), ())), preferred_element_type=F32).astype(BF)
    for s in range(4):
        dzn[T * s : T * s + T] = turned[:, T * s : T * s + T]
    both = jnp.concatenate([x, agg], axis=1)
    grads = lax.dot_general(both, dz, (((0,), (0,)), ((), ())), preferred_element_type=F32)
    column = jnp.sum(dz.astype(F32), axis=0, keepdims=True)
    for y in range(4):
        gbuf[y, 0:64] = grads[64 * y : 64 * y + 64, 0:T].astype(BF)
        gbuf[y, 64:128] = grads[64 * y : 64 * y + 64, T : 2 * T].astype(BF)
    columns = jnp.concatenate([column[:, 0:T], column[:, T : 2 * T]], axis=0)
    high = columns.astype(BF)
    low = (columns - high.astype(F32)).astype(BF)
    tail = jnp.concatenate([high.astype(F32), low.astype(F32), jnp.zeros((12, T), F32)], axis=0).astype(BF)
    for k, pay in ((0, own_w), (1, pay1), (2, pay2), (3, pay3)):
        offset = 0
        if k:
            pay[0 : 4 * T] = dzn[...]
            offset = 4 * T
        pay[offset : offset + T] = gbuf[my_first[0] ^ k]
        pay[offset + T : offset + T + 16] = tail
    base[...] = lax.dot_general(dz, w_self[...], (((1,), (1,)), ((), ())), preferred_element_type=F32)


def layer(my_first, parts, feats, w_self, w_neigh, bias, cot):
    rows = feats.shape[0]
    pay = shape(rows + T + 16, T, BF)
    return pl.pallas_call(
        layer_kernel,
        out_shape=[shape(rows, 2 * T, BF), shape(rows, T, F32), shape(rows, T, BF), pay, pay, pay, shape(T + 16, T, BF)],
        in_specs=[SM] + [VM] * 9,
        out_specs=[VM] * 7,
        scratch_shapes=[pltpu.VMEM((4, T, T), BF)],
        compiler_params=pltpu.CompilerParams(vmem_limit_bytes=VMEM_LIMIT),
        name="layer",
    )(my_first, *parts, feats, w_self, w_neigh, bias, cot)


def weights_kernel(firsts, scale, *refs):
    chunks, (g_self, g_neigh, g_bias, mine, theirs) = refs[:8], refs[8:]
    for core, whole in ((0, mine), (1, theirs)):
        for k in range(4):
            c = chunks[4 * core + k]
            at = pl.ds(pl.multiple_of((firsts[core] ^ k) * 64, 64), 64)
            whole[at, 0:T] = c[0:64]
            whole[at, T : 2 * T] = c[64:128]
    total = (mine[...] + theirs[...]) * scale[0]
    g_self[...] = total[0:T]
    g_neigh[...] = total[T : 2 * T]
    a, b = chunks[0], chunks[4]
    g_bias[...] = ((a[T : T + 2] + a[T + 2 : T + 4]) + (b[T : T + 2] + b[T + 2 : T + 4])) * scale[0]


def weights(firsts, scale, chunks):
    return pl.pallas_call(
        weights_kernel,
        out_shape=[shape(T, 2 * T, F32), shape(T, 2 * T, F32), shape(2, T, F32)],
        in_specs=[SM, SM] + [VM] * 8,
        out_specs=[VM] * 3,
        scratch_shapes=[pltpu.VMEM((2 * T, 2 * T), F32)] * 2,
        name="weights",
    )(firsts, scale, *chunks)


def finish_kernel(base, p0, f1, b1, f2, b2, grad):
    for s in range(4):
        spread = (
            p0[s] + (f1[s].astype(F32) + b1[s].astype(F32)) + (f2[s].astype(F32) + b2[s].astype(F32))
        )
        grad[T * s : T * s + T] = base[T * s : T * s + T] + spread.T


def finish(base, p0, f1, b1, f2, b2):
    return pl.pallas_call(
        finish_kernel,
        out_shape=shape(base.shape[0], T, F32),
        in_specs=[VM] * 6,
        out_specs=VM,
        cost_estimate=pl.CostEstimate(flops=10**10, bytes_accessed=2**20, transcendentals=0),
        name="finish",
    )(base, p0, f1, b1, f2, b2)


def wide_sum(values):
    values = [value.astype(F32) for value in values]
    return (values[0] + values[1]) + (values[2] + values[3])


def per_device(feats, w_self, w_neigh, bias, tiles, tile_row, tile_col, tile_count, cotangent):
    rows_dev, width = feats.shape
    total_nodes = rows_dev * 256
    tiles = tiles.reshape(SLOTS, T, T)
    my_z = lax.axis_index("row")
    my_rep = lax.axis_index("rep")
    my_x, my_y, my_c = my_rep // 8, (my_rep // 2) % 4, my_rep % 2
    firsts = jnp.where(my_c == 0, jnp.stack([my_x, my_y]), jnp.stack([my_y, my_x]))
    count = tile_count.reshape(1)
    live = jnp.arange(SLOTS, dtype=jnp.int32) < count
    row = tile_row.reshape(SLOTS)
    col = tile_col.reshape(SLOTS)

    owner, sub = row // 4, row % 4
    kx, ky, kc = (owner // 8) ^ my_x, ((owner // 2) % 4) ^ my_y, (owner % 2) ^ my_c
    k1, k2 = jnp.where(owner % 2 == 0, kx, ky), jnp.where(owner % 2 == 0, ky, kx)
    slab_place = jnp.where(live, 64 * (1 - kc) + (k1 * 4 + k2) * 4 + sub, 128)
    slab_source = 64 * kc + (k2 * 4 + k1) * 4 + sub
    col_block = ((col // 4 - my_z) % 8) * 4 + col % 4
    section_place = jnp.where(live, col_block, 32)

    up2, down2 = row_move(feats, 2), row_move(feats, -2)
    up1, down1 = row_move(feats, 1), row_move(feats, -1)
    up4, down4 = row_move(up2[: rows_dev // 2], 2), row_move(down2[rows_dev // 2 :], -2)
    up3, down3 = row_move(up2, 1), row_move(down2, -1)
    blocks = [feats, down1, down2, down3, up4, up3, up2, up1, down4]
    blocks = [block.reshape(-1, T, T) for block in blocks]

    parts = forward(count, slab_place, col_block, tiles, blocks)
    both = [None] * 4
    for k in (2, 1, 3, 0):
        both[k] = parts[4 + k].astype(F32) + other_core(parts[k]).astype(F32)
    got = [axis_move(both[k].astype(BF), 0, k) for k in (2, 1, 3)]
    total = wide_sum([both[0]] + got)
    parts = [total[0:4]] + [axis_move(total[4 * k : 4 * k + 4].astype(BF), 1, k) for k in (1, 2, 3)]
    parts = [part.reshape(rows_dev, T) for part in parts]

    out, base, dzn, pay1, pay2, pay3, own_w = layer(
        firsts[:1], parts, feats, w_self, w_neigh, bias.reshape(1, -1), cotangent
    )

    got = [None] * 4
    for k, pay in ((2, pay2), (1, pay1), (3, pay3)):
        got[k] = axis_move(pay, 0, k)
    gw = wide_sum([own_w] + [got[k][rows_dev:] for k in (1, 2, 3)]).astype(BF)
    bundle = jnp.concatenate([dzn] + [got[k][:rows_dev] for k in (1, 2, 3)] + [gw], axis=0)
    own = [bundle, None, None, None]
    for k in (2, 1, 3):
        own[k] = axis_move(bundle, 1, k)
    far = [other_core(v) for v in own]
    gw = wide_sum([v[4 * rows_dev :] for v in own]).astype(BF)
    swapped = row_swap(gw, 1)

    p = backward(count, section_place, slab_source, tiles, own + far)
    gw, swapped, p = lax.optimization_barrier((gw, swapped, p))
    gw = (gw.astype(F32) + swapped.astype(F32)).astype(BF)
    up3, down3 = row_move(p[3], 1), row_move(p[5], -1)
    up4, down4 = row_move(p[4], 2), row_move(p[8], -2)
    swapped = row_swap(gw, 4)
    up3, down3, up4, down4, swapped, gw, p = lax.optimization_barrier((up3, down3, up4, down4, swapped, gw, p))
    zeros = jnp.zeros((2, T, T), F32)
    up2 = p[2].astype(F32) + up3.astype(F32) + jnp.concatenate([up4.astype(F32), zeros], axis=0)
    down2 = p[6].astype(F32) + down3.astype(F32) + jnp.concatenate([zeros, down4.astype(F32)], axis=0)
    up2, down2 = row_move(up2.astype(BF), 2), row_move(down2.astype(BF), -2)
    up1, down1 = row_move(p[1], 1), row_move(p[7], -1)
    grad_feats = finish(base, p[0], up1, down1, up2, down2)

    gw = (gw.astype(F32) + swapped.astype(F32)).astype(BF)
    gw = gw.astype(F32) + row_swap(gw, 2).astype(F32)
    quarters = [gw] + [axis_move(gw, 0, k) for k in (1, 2, 3)]
    quarters += [other_core(quarter) for quarter in quarters]
    scale = (1.0 / jnp.sqrt(jnp.float32(total_nodes))).reshape(1)
    grad_self, grad_neigh, grad_bias = weights(firsts, scale, quarters)
    return out, grad_feats, grad_self, grad_neigh, grad_bias.reshape(-1)


def solution(mesh):
    placed = (
        P(("row", "rep"), None),
        P(),
        P(),
        P(),
        P("row", "rep", None, None, None),
        P("row", "rep", None),
        P("row", "rep", None),
        P("row", "rep"),
        P(("row", "rep"), None),
    )
    return jax.shard_map(
        per_device,
        mesh=mesh,
        in_specs=placed,
        out_specs=(P(("row", "rep"), None), P(("row", "rep"), None), P(), P(), P()),
        check_vma=False,
    )
```

```python
import jax
import jax.numpy as jnp
from jax import lax
from jax.experimental import pallas as pl
from jax.experimental.pallas import tpu as pltpu
from jax.sharding import PartitionSpec as P

T = 128
SLOTS = 256
CHUNK = 8
GROUP = 4
HALF = 2 * T + 16
BF = jnp.bfloat16
F32 = jnp.float32
VMEM_LIMIT = 48 * 1024 * 1024

VM = pl.BlockSpec(memory_space=pltpu.VMEM)
SM = pl.BlockSpec(memory_space=pltpu.SMEM)
HB = pl.BlockSpec(memory_space=pl.ANY)


def shape(rows, cols, dtype):
    return jax.ShapeDtypeStruct((rows, cols), dtype)


def other_core(value):
    return lax.ppermute(value, "rep", [(i, i ^ 1) for i in range(32)])


def axis_move(value, which, k):
    return lax.ppermute(value, "rep", [(i, i ^ (k * (8 if i % 2 == which else 2))) for i in range(32)])


def row_move(value, step):
    return lax.ppermute(value, "row", [(i, (i + step) % 8) for i in range(8)])


def row_swap(value, bit):
    return lax.ppermute(value, "row", [(i, i ^ bit) for i in range(8)])


def tile_copy(tiles, tbuf, sem, i):
    part = pl.ds(pl.multiple_of(i * CHUNK, CHUNK), CHUNK)
    return pltpu.make_async_copy(tiles.at[part], tbuf.at[part], sem.at[i])


def start_tiles(count, tiles, tbuf, sem):
    chunks = (count[0] + CHUNK - 1) // CHUNK

    def start(i, carry):
        tile_copy(tiles, tbuf, sem, i).start()
        return carry

    lax.fori_loop(0, chunks, start, 0)
    return chunks


def zero(acc):
    def clear(i, carry):
        acc[i] = jnp.zeros((T, T), F32)
        return carry

    lax.fori_loop(0, acc.shape[0], clear, 0, unroll=4)


def add_products(chunks, tiles, tbuf, sem, product, place, acc):
    def step(i, carry):
        tile_copy(tiles, tbuf, sem, i).wait()
        for g in range(0, CHUNK, GROUP):
            slots = [i * CHUNK + g + k for k in range(GROUP)]
            prods = [product(t) for t in slots]
            for t, prod in zip(slots, prods):
                q = place[t]
                acc[q] = acc[q] + prod
        return carry

    lax.fori_loop(0, chunks, step, 0)


def forward_kernel(count, place, source, tiles, *rest):
    feats, outs = rest[:9], rest[9:17]
    tbuf, fbuf, acc, stage, tsem, fsem, osem = rest[17:]
    loads = []
    for d in range(8):
        if d == 4:
            loads.append(pltpu.make_async_copy(feats[4], fbuf.at[pl.ds(16, 2)], fsem.at[4]))
            loads.append(pltpu.make_async_copy(feats[8], fbuf.at[pl.ds(18, 2)], fsem.at[8]))
        else:
            loads.append(pltpu.make_async_copy(feats[d], fbuf.at[pl.ds(4 * d, 4)], fsem.at[d]))
    for load in loads:
        load.start()
    chunks = start_tiles(count, tiles, tbuf, tsem)
    zero(acc)
    for load in loads:
        load.wait()

    def product(t):
        return jnp.dot(tbuf[t], fbuf[source[t]], preferred_element_type=F32)

    add_products(chunks, tiles, tbuf, tsem, product, place, acc)
    stores = []
    for k in range(8):
        part = pl.ds(16 * k, 16)
        stage[part] = acc[part].astype(BF)
        stores.append(pltpu.make_async_copy(stage.at[part], outs[k], osem.at[k]))
        stores[-1].start()
    for store in stores:
        store.wait()


def forward(count, place, source, tiles, feats):
    blocks = [jax.ShapeDtypeStruct((16, T, T), BF)] * 8
    return pl.pallas_call(
        forward_kernel,
        out_shape=blocks,
        in_specs=[SM, SM, SM, HB] + [HB] * 9,
        out_specs=[HB] * 8,
        scratch_shapes=[
            pltpu.VMEM((SLOTS, T, T), BF),
            pltpu.VMEM((32, T, T), BF),
            pltpu.VMEM((129, T, T), F32),
            pltpu.VMEM((128, T, T), BF),
            pltpu.SemaphoreType.DMA((SLOTS // CHUNK,)),
            pltpu.SemaphoreType.DMA((9,)),
            pltpu.SemaphoreType.DMA((8,)),
        ],
        compiler_params=pltpu.CompilerParams(vmem_limit_bytes=VMEM_LIMIT),
        cost_estimate=pl.CostEstimate(flops=2 * SLOTS * T**3, bytes_accessed=16 * 2**20, transcendentals=0),
        name="tiles_forward",
    )(count, place, source, tiles, *feats)


def backward_kernel(count, place, source, tiles, *rest):
    grads, outs = rest[:8], rest[8:17]
    tbuf, gbuf, acc, stage, tsem, gsem, osem = rest[17:]
    loads = [
        pltpu.make_async_copy(grads[k].at[pl.ds(0, 16 * T)], gbuf.at[pl.ds(16 * T * k, 16 * T)], gsem.at[k])
        for k in range(8)
    ]
    for load in loads:
        load.start()
    chunks = start_tiles(count, tiles, tbuf, tsem)
    zero(acc)
    for load in loads:
        load.wait()

    def product(t):
        grad = gbuf[pl.ds(pl.multiple_of(source[t] * T, T), T)]
        return jnp.dot(grad, tbuf[t], preferred_element_type=F32)

    add_products(chunks, tiles, tbuf, tsem, product, place, acc)
    stores = [pltpu.make_async_copy(acc.at[pl.ds(0, 4)], outs[0], osem.at[0])]
    stores[0].start()
    for d in range(1, 8):
        stage[pl.ds(4 * d, 4)] = acc[pl.ds(4 * d, 4)].astype(BF)
        if d == 4:
            stores.append(pltpu.make_async_copy(stage.at[pl.ds(16, 2)], outs[4], osem.at[4]))
            stores.append(pltpu.make_async_copy(stage.at[pl.ds(18, 2)], outs[8], osem.at[8]))
            stores[-2].start()
        else:
            stores.append(pltpu.make_async_copy(stage.at[pl.ds(4 * d, 4)], outs[d], osem.at[d]))
        stores[-1].start()
    for store in stores:
        store.wait()


def backward(count, place, source, tiles, grads):
    four = jax.ShapeDtypeStruct((4, T, T), BF)
    two = jax.ShapeDtypeStruct((2, T, T), BF)
    outs = [jax.ShapeDtypeStruct((4, T, T), F32), four, four, four, two, four, four, four, two]
    return pl.pallas_call(
        backward_kernel,
        out_shape=outs,
        in_specs=[SM, SM, SM, HB] + [HB] * 8,
        out_specs=[HB] * 9,
        scratch_shapes=[
            pltpu.VMEM((SLOTS, T, T), BF),
            pltpu.VMEM((128 * T, T), BF),
            pltpu.VMEM((33, T, T), F32),
            pltpu.VMEM((32, T, T), BF),
            pltpu.SemaphoreType.DMA((SLOTS // CHUNK,)),
            pltpu.SemaphoreType.DMA((8,)),
            pltpu.SemaphoreType.DMA((9,)),
        ],
        compiler_params=pltpu.CompilerParams(vmem_limit_bytes=VMEM_LIMIT),
        cost_estimate=pl.CostEstimate(flops=2 * SLOTS * T**3, bytes_accessed=16 * 2**20, transcendentals=0),
        name="tiles_backward",
    )(count, place, source, tiles, *grads)


def layer_kernel(core, a0, a1, a2, a3, feats, w_self, w_neigh, bias, cot, out, base, dzn, keep, give, halves):
    agg = (a0[...] + a1[...].astype(F32)) + (a2[...].astype(F32) + a3[...].astype(F32))
    agg = agg.astype(BF)
    x = feats[...]
    z = (
        jnp.dot(x, w_self[...], preferred_element_type=F32)
        + jnp.dot(agg, w_neigh[...], preferred_element_type=F32)
        + bias[...]
    )
    root = 0.7978845608028654
    t = jnp.tanh(root * (z + 0.044715 * (z * z * z)))
    cdf = 0.5 * (1.0 + t)
    out[...] = (z * cdf).astype(BF)
    slope = cdf + 0.5 * z * (1.0 - t * t) * (root * (1.0 + 3.0 * 0.044715 * (z * z)))
    dz = (cot[...].astype(F32) * slope).astype(BF)
    turned = lax.dot_general(w_neigh[...], dz, (((1,), (1,)), ((), ())), preferred_element_type=F32).astype(BF)
    for s in range(4):
        dzn[T * s : T * s + T] = turned[:, T * s : T * s + T]
    both = jnp.concatenate([x, agg], axis=1)
    grads = lax.dot_general(both, dz, (((0,), (0,)), ((), ())), preferred_element_type=F32).astype(BF)
    column = jnp.sum(dz.astype(F32), axis=0, keepdims=True)
    columns = jnp.concatenate([column[:, 0:T], column[:, T : 2 * T]], axis=0)
    high = columns.astype(BF).astype(F32)
    tail = jnp.concatenate([high, columns - high, jnp.zeros((12, T), F32)], axis=0).astype(BF)
    for m in range(2):
        halves[m, 0:T] = grads[T * m : T * m + T, 0:T]
        halves[m, T : 2 * T] = grads[T * m : T * m + T, T : 2 * T]
        halves[m, 2 * T : HALF] = tail
    keep[...] = halves[core[0]]
    give[...] = halves[1 - core[0]]
    base[...] = lax.dot_general(dz, w_self[...], (((1,), (1,)), ((), ())), preferred_element_type=F32)


def layer(core, parts, feats, w_self, w_neigh, bias, cot):
    rows = feats.shape[0]
    half = shape(HALF, T, BF)
    return pl.pallas_call(
        layer_kernel,
        out_shape=[shape(rows, 2 * T, BF), shape(rows, T, F32), shape(rows, T, BF), half, half],
        in_specs=[SM] + [VM] * 9,
        out_specs=[VM] * 5,
        scratch_shapes=[pltpu.VMEM((2, HALF, T), BF)],
        compiler_params=pltpu.CompilerParams(vmem_limit_bytes=VMEM_LIMIT),
        name="layer",
    )(core, *parts, feats, w_self, w_neigh, bias, cot)


def finish_kernel(core, scale, base, p0, f1, b1, f2, b2, mine, theirs, grad, g_self, g_neigh, g_bias):
    for s in range(4):
        spread = (
            p0[s] + (f1[s].astype(F32) + b1[s].astype(F32)) + (f2[s].astype(F32) + b2[s].astype(F32))
        )
        grad[T * s : T * s + T] = base[T * s : T * s + T] + spread.T
    first = core[0] == 0
    own, other = mine[...] * scale[0], theirs[...] * scale[0]
    low, high = jnp.where(first, own, other), jnp.where(first, other, own)
    for g, part in ((g_self, low), (g_neigh, high)):
        g[:, 0:T] = part[0:T]
        g[:, T : 2 * T] = part[T : 2 * T]
    g_bias[...] = low[2 * T : 2 * T + 2] + low[2 * T + 2 : 2 * T + 4]


def finish(core, scale, base, p0, f1, b1, f2, b2, mine, theirs):
    return pl.pallas_call(
        finish_kernel,
        out_shape=[
            shape(base.shape[0], T, F32), shape(T, 2 * T, F32), shape(T, 2 * T, F32), shape(2, T, F32)
        ],
        in_specs=[SM, SM] + [VM] * 8,
        out_specs=[VM] * 4,
        name="finish",
    )(core, scale, base, p0, f1, b1, f2, b2, mine, theirs)


def wide_sum(values):
    values = [value.astype(F32) for value in values]
    return (values[0] + values[1]) + (values[2] + values[3])


def per_device(feats, w_self, w_neigh, bias, tiles, tile_row, tile_col, tile_count, cotangent):
    rows_dev, width = feats.shape
    total_nodes = rows_dev * 256
    tiles = tiles.reshape(SLOTS, T, T)
    my_z = lax.axis_index("row")
    my_rep = lax.axis_index("rep")
    my_x, my_y, my_c = my_rep // 8, (my_rep // 2) % 4, my_rep % 2
    count = tile_count.reshape(1)
    live = jnp.arange(SLOTS, dtype=jnp.int32) < count
    row = tile_row.reshape(SLOTS)
    col = tile_col.reshape(SLOTS)

    owner, sub = row // 4, row % 4
    kx, ky, kc = (owner // 8) ^ my_x, ((owner // 2) % 4) ^ my_y, (owner % 2) ^ my_c
    k1, k2 = jnp.where(owner % 2 == 0, kx, ky), jnp.where(owner % 2 == 0, ky, kx)
    slab_place = jnp.where(live, 64 * (1 - kc) + (k1 * 4 + k2) * 4 + sub, 128)
    slab_source = 64 * kc + (k2 * 4 + k1) * 4 + sub
    col_block = ((col // 4 - my_z) % 8) * 4 + col % 4
    section_place = jnp.where(live, col_block, 32)

    up2, down2 = row_move(feats, 2), row_move(feats, -2)
    up1, down1 = row_move(feats, 1), row_move(feats, -1)
    up4, down4 = row_move(up2[: rows_dev // 2], 2), row_move(down2[rows_dev // 2 :], -2)
    up3, down3 = row_move(up2, 1), row_move(down2, -1)
    blocks = [feats, down1, down2, down3, up4, up3, up2, up1, down4]
    blocks = [block.reshape(-1, T, T) for block in blocks]

    parts = forward(count, slab_place, col_block, tiles, blocks)
    both = [None] * 4
    for k in (2, 1, 3, 0):
        both[k] = parts[4 + k].astype(F32) + other_core(parts[k]).astype(F32)
    got = [axis_move(both[k].astype(BF), 0, k) for k in (2, 1, 3)]
    total = wide_sum([both[0]] + got)
    parts = [total[0:4]] + [axis_move(total[4 * k : 4 * k + 4].astype(BF), 1, k) for k in (1, 2, 3)]
    parts = [part.reshape(rows_dev, T) for part in parts]

    core = my_c.reshape(1)
    out, base, dzn, keep, give = layer(core, parts, feats, w_self, w_neigh, bias.reshape(1, -1), cotangent)

    half = (keep.astype(F32) + other_core(give).astype(F32)).astype(BF)
    pay = jnp.concatenate([dzn, half], axis=0)
    got = [pay, None, None, None]
    for k in (2, 1, 3):
        got[k] = axis_move(pay, 0, k)
    gw = wide_sum([v[rows_dev:] for v in got]).astype(BF)
    bundle = jnp.concatenate([v[:rows_dev] for v in got] + [gw], axis=0)
    own = [bundle, None, None, None]
    for k in (2, 1, 3):
        own[k] = axis_move(bundle, 1, k)
    far = [other_core(v) for v in own]
    gw = wide_sum([v[4 * rows_dev :] for v in own]).astype(BF)
    swapped = [row_swap(gw, bits) for bits in (1, 4, 5)]

    p = backward(count, section_place, slab_source, tiles, own + far)
    gw, swapped, p = lax.optimization_barrier((gw, swapped, p))
    gw = wide_sum([gw] + swapped).astype(BF)
    up3, down3 = row_move(p[3], 1), row_move(p[5], -1)
    up4, down4 = row_move(p[4], 2), row_move(p[8], -2)
    swapped = row_swap(gw, 2)
    up3, down3, up4, down4, p = lax.optimization_barrier((up3, down3, up4, down4, p))
    zeros = jnp.zeros((2, T, T), F32)
    up2 = p[2].astype(F32) + up3.astype(F32) + jnp.concatenate([up4.astype(F32), zeros], axis=0)
    down2 = p[6].astype(F32) + down3.astype(F32) + jnp.concatenate([zeros, down4.astype(F32)], axis=0)
    up2, down2 = row_move(up2.astype(BF), 2), row_move(down2.astype(BF), -2)
    up1, down1 = row_move(p[1], 1), row_move(p[7], -1)
    gw = gw.astype(F32) + swapped.astype(F32)
    scale = (1.0 / jnp.sqrt(jnp.float32(total_nodes))).reshape(1)
    grad_feats, grad_self, grad_neigh, grad_bias = finish(
        core, scale, base, p[0], up1, down1, up2, down2, gw, other_core(gw)
    )
    return out, grad_feats, grad_self, grad_neigh, grad_bias.reshape(-1)


def solution(mesh):
    placed = (
        P(("row", "rep"), None),
        P(),
        P(),
        P(),
        P("row", "rep", None, None, None),
        P("row", "rep", None),
        P("row", "rep", None),
        P("row", "rep"),
        P(("row", "rep"), None),
    )
    return jax.shard_map(
        per_device,
        mesh=mesh,
        in_specs=placed,
        out_specs=(P(("row", "rep"), None), P(("row", "rep"), None), P(), P(), P()),
        check_vma=False,
    )
```

```python
import jax
import jax.numpy as jnp
from jax import lax
from jax.experimental import pallas as pl
from jax.experimental.pallas import tpu as pltpu
from jax.sharding import PartitionSpec as P

T = 128
SLOTS = 256
CHUNK = 8
GROUP = 4
HALF = 2 * T + 16
BF = jnp.bfloat16
F32 = jnp.float32
VMEM_LIMIT = 48 * 1024 * 1024

VM = pl.BlockSpec(memory_space=pltpu.VMEM)
SM = pl.BlockSpec(memory_space=pltpu.SMEM)
HB = pl.BlockSpec(memory_space=pl.ANY)


def shape(rows, cols, dtype):
    return jax.ShapeDtypeStruct((rows, cols), dtype)


def other_core(value):
    return lax.ppermute(value, "rep", [(i, i ^ 1) for i in range(32)])


def axis_move(value, which, k):
    return lax.ppermute(value, "rep", [(i, i ^ (k * (8 if i % 2 == which else 2))) for i in range(32)])


def row_move(value, step):
    return lax.ppermute(value, "row", [(i, (i + step) % 8) for i in range(8)])


def row_swap(value, bit):
    return lax.ppermute(value, "row", [(i, i ^ bit) for i in range(8)])


def tile_copy(tiles, tbuf, sem, i):
    part = pl.ds(pl.multiple_of(i * CHUNK, CHUNK), CHUNK)
    return pltpu.make_async_copy(tiles.at[part], tbuf.at[part], sem.at[i])


def start_tiles(count, tiles, tbuf, sem):
    chunks = (count[0] + CHUNK - 1) // CHUNK

    def start(i, carry):
        tile_copy(tiles, tbuf, sem, i).start()
        return carry

    lax.fori_loop(0, chunks, start, 0)
    return chunks


def zero(acc):
    def clear(i, carry):
        acc[i] = jnp.zeros((T, T), F32)
        return carry

    lax.fori_loop(0, acc.shape[0], clear, 0, unroll=4)


def add_products(chunks, tiles, tbuf, sem, product, place, acc):
    def step(i, carry):
        tile_copy(tiles, tbuf, sem, i).wait()
        for g in range(0, CHUNK, GROUP):
            slots = [i * CHUNK + g + k for k in range(GROUP)]
            prods = [product(t) for t in slots]
            for t, prod in zip(slots, prods):
                q = place[t]
                acc[q] = acc[q] + prod
        return carry

    lax.fori_loop(0, chunks, step, 0)


def forward_kernel(count, place, source, tiles, *rest):
    feats, outs = rest[:9], rest[9:17]
    tbuf, fbuf, acc, stage, tsem, fsem, osem = rest[17:]
    loads = []
    for d in range(8):
        if d == 4:
            loads.append(pltpu.make_async_copy(feats[4], fbuf.at[pl.ds(16, 2)], fsem.at[4]))
            loads.append(pltpu.make_async_copy(feats[8], fbuf.at[pl.ds(18, 2)], fsem.at[8]))
        else:
            loads.append(pltpu.make_async_copy(feats[d], fbuf.at[pl.ds(4 * d, 4)], fsem.at[d]))
    for load in loads:
        load.start()
    chunks = start_tiles(count, tiles, tbuf, tsem)
    zero(acc)
    for load in loads:
        load.wait()

    def product(t):
        return jnp.dot(tbuf[t], fbuf[source[t]], preferred_element_type=F32)

    add_products(chunks, tiles, tbuf, tsem, product, place, acc)
    stores = []
    for k in range(8):
        part = pl.ds(16 * k, 16)
        stage[part] = acc[part].astype(BF)
        stores.append(pltpu.make_async_copy(stage.at[part], outs[k], osem.at[k]))
        stores[-1].start()
    for store in stores:
        store.wait()


def forward(count, place, source, tiles, feats):
    blocks = [jax.ShapeDtypeStruct((16, T, T), BF)] * 8
    return pl.pallas_call(
        forward_kernel,
        out_shape=blocks,
        in_specs=[SM, SM, SM, HB] + [HB] * 9,
        out_specs=[HB] * 8,
        scratch_shapes=[
            pltpu.VMEM((SLOTS, T, T), BF),
            pltpu.VMEM((32, T, T), BF),
            pltpu.VMEM((129, T, T), F32),
            pltpu.VMEM((128, T, T), BF),
            pltpu.SemaphoreType.DMA((SLOTS // CHUNK,)),
            pltpu.SemaphoreType.DMA((9,)),
            pltpu.SemaphoreType.DMA((8,)),
        ],
        compiler_params=pltpu.CompilerParams(vmem_limit_bytes=VMEM_LIMIT),
        cost_estimate=pl.CostEstimate(flops=2 * SLOTS * T**3, bytes_accessed=16 * 2**20, transcendentals=0),
        name="tiles_forward",
    )(count, place, source, tiles, *feats)


def backward_kernel(count, place, source, tiles, *rest):
    grads, outs = rest[:8], rest[8:17]
    tbuf, gbuf, acc, stage, tsem, gsem, osem = rest[17:]
    loads = [
        pltpu.make_async_copy(grads[k].at[pl.ds(0, 16 * T)], gbuf.at[pl.ds(16 * T * k, 16 * T)], gsem.at[k])
        for k in range(8)
    ]
    for load in loads:
        load.start()
    chunks = start_tiles(count, tiles, tbuf, tsem)
    zero(acc)
    for load in loads:
        load.wait()

    def product(t):
        grad = gbuf[pl.ds(pl.multiple_of(source[t] * T, T), T)]
        return jnp.dot(grad, tbuf[t], preferred_element_type=F32)

    add_products(chunks, tiles, tbuf, tsem, product, place, acc)
    stores = [pltpu.make_async_copy(acc.at[pl.ds(0, 4)], outs[0], osem.at[0])]
    stores[0].start()
    for d in range(1, 8):
        stage[pl.ds(4 * d, 4)] = acc[pl.ds(4 * d, 4)].astype(BF)
        if d == 4:
            stores.append(pltpu.make_async_copy(stage.at[pl.ds(16, 2)], outs[4], osem.at[4]))
            stores.append(pltpu.make_async_copy(stage.at[pl.ds(18, 2)], outs[8], osem.at[8]))
            stores[-2].start()
        else:
            stores.append(pltpu.make_async_copy(stage.at[pl.ds(4 * d, 4)], outs[d], osem.at[d]))
        stores[-1].start()
    for store in stores:
        store.wait()


def backward(count, place, source, tiles, grads):
    four = jax.ShapeDtypeStruct((4, T, T), BF)
    two = jax.ShapeDtypeStruct((2, T, T), BF)
    outs = [jax.ShapeDtypeStruct((4, T, T), F32), four, four, four, two, four, four, four, two]
    return pl.pallas_call(
        backward_kernel,
        out_shape=outs,
        in_specs=[SM, SM, SM, HB] + [HB] * 8,
        out_specs=[HB] * 9,
        scratch_shapes=[
            pltpu.VMEM((SLOTS, T, T), BF),
            pltpu.VMEM((128 * T, T), BF),
            pltpu.VMEM((33, T, T), F32),
            pltpu.VMEM((32, T, T), BF),
            pltpu.SemaphoreType.DMA((SLOTS // CHUNK,)),
            pltpu.SemaphoreType.DMA((8,)),
            pltpu.SemaphoreType.DMA((9,)),
        ],
        compiler_params=pltpu.CompilerParams(vmem_limit_bytes=VMEM_LIMIT),
        cost_estimate=pl.CostEstimate(flops=2 * SLOTS * T**3, bytes_accessed=16 * 2**20, transcendentals=0),
        name="tiles_backward",
    )(count, place, source, tiles, *grads)


def layer_kernel(core, a0, a1, a2, a3, feats, w_self, w_neigh, bias, cot, out, base, dzn, keep, give, halves):
    agg = (a0[...] + a1[...].astype(F32)) + (a2[...].astype(F32) + a3[...].astype(F32))
    agg = agg.astype(BF)
    x = feats[...]
    z = (
        jnp.dot(x, w_self[...], preferred_element_type=F32)
        + jnp.dot(agg, w_neigh[...], preferred_element_type=F32)
        + bias[...]
    )
    root = 0.7978845608028654
    t = jnp.tanh(root * (z + 0.044715 * (z * z * z)))
    cdf = 0.5 * (1.0 + t)
    out[...] = (z * cdf).astype(BF)
    slope = cdf + 0.5 * z * (1.0 - t * t) * (root * (1.0 + 3.0 * 0.044715 * (z * z)))
    dz = (cot[...].astype(F32) * slope).astype(BF)
    turned = lax.dot_general(w_neigh[...], dz, (((1,), (1,)), ((), ())), preferred_element_type=F32).astype(BF)
    for s in range(4):
        dzn[T * s : T * s + T] = turned[:, T * s : T * s + T]
    both = jnp.concatenate([x, agg], axis=1)
    grads = lax.dot_general(both, dz, (((0,), (0,)), ((), ())), preferred_element_type=F32).astype(BF)
    column = jnp.sum(dz.astype(F32), axis=0, keepdims=True)
    columns = jnp.concatenate([column[:, 0:T], column[:, T : 2 * T]], axis=0)
    high = columns.astype(BF).astype(F32)
    tail = jnp.concatenate([high, columns - high, jnp.zeros((12, T), F32)], axis=0).astype(BF)
    for m in range(2):
        halves[m, 0:T] = grads[T * m : T * m + T, 0:T]
        halves[m, T : 2 * T] = grads[T * m : T * m + T, T : 2 * T]
        halves[m, 2 * T : HALF] = tail
    keep[...] = halves[core[0]]
    give[...] = halves[1 - core[0]]
    base[...] = lax.dot_general(dz, w_self[...], (((1,), (1,)), ((), ())), preferred_element_type=F32)


def layer(core, parts, feats, w_self, w_neigh, bias, cot):
    rows = feats.shape[0]
    half = shape(HALF, T, BF)
    return pl.pallas_call(
        layer_kernel,
        out_shape=[shape(rows, 2 * T, BF), shape(rows, T, F32), shape(rows, T, BF), half, half],
        in_specs=[SM] + [VM] * 9,
        out_specs=[VM] * 5,
        scratch_shapes=[pltpu.VMEM((2, HALF, T), BF)],
        compiler_params=pltpu.CompilerParams(vmem_limit_bytes=VMEM_LIMIT),
        name="layer",
    )(core, *parts, feats, w_self, w_neigh, bias, cot)


def finish_kernel(core, scale, base, p0, f1, b1, f2, b2, mine, theirs, grad, g_self, g_neigh, g_bias):
    for s in range(4):
        spread = (
            p0[s] + (f1[s].astype(F32) + b1[s].astype(F32)) + (f2[s].astype(F32) + b2[s].astype(F32))
        )
        grad[T * s : T * s + T] = base[T * s : T * s + T] + spread.T
    first = core[0] == 0
    own, other = mine[...] * scale[0], theirs[...] * scale[0]
    low, high = jnp.where(first, own, other), jnp.where(first, other, own)
    for g, part in ((g_self, low), (g_neigh, high)):
        g[:, 0:T] = part[0:T]
        g[:, T : 2 * T] = part[T : 2 * T]
    g_bias[...] = low[2 * T : 2 * T + 2] + low[2 * T + 2 : 2 * T + 4]


def finish(core, scale, base, p0, f1, b1, f2, b2, mine, theirs):
    return pl.pallas_call(
        finish_kernel,
        out_shape=[
            shape(base.shape[0], T, F32), shape(T, 2 * T, F32), shape(T, 2 * T, F32), shape(2, T, F32)
        ],
        in_specs=[SM, SM] + [VM] * 8,
        out_specs=[VM] * 4,
        name="finish",
    )(core, scale, base, p0, f1, b1, f2, b2, mine, theirs)


def wide_sum(values):
    values = [value.astype(F32) for value in values]
    return (values[0] + values[1]) + (values[2] + values[3])


def per_device(feats, w_self, w_neigh, bias, tiles, tile_row, tile_col, tile_count, cotangent):
    rows_dev, width = feats.shape
    total_nodes = rows_dev * 256
    tiles = tiles.reshape(SLOTS, T, T)
    my_z = lax.axis_index("row")
    my_rep = lax.axis_index("rep")
    my_x, my_y, my_c = my_rep // 8, (my_rep // 2) % 4, my_rep % 2
    count = tile_count.reshape(1)
    live = jnp.arange(SLOTS, dtype=jnp.int32) < count
    row = tile_row.reshape(SLOTS)
    col = tile_col.reshape(SLOTS)

    owner, sub = row // 4, row % 4
    kx, ky, kc = (owner // 8) ^ my_x, ((owner // 2) % 4) ^ my_y, (owner % 2) ^ my_c
    k1, k2 = jnp.where(owner % 2 == 0, kx, ky), jnp.where(owner % 2 == 0, ky, kx)
    slab_place = jnp.where(live, 64 * (1 - kc) + (k1 * 4 + k2) * 4 + sub, 128)
    slab_source = 64 * kc + (k2 * 4 + k1) * 4 + sub
    col_block = ((col // 4 - my_z) % 8) * 4 + col % 4
    section_place = jnp.where(live, col_block, 32)

    up2, down2 = row_move(feats, 2), row_move(feats, -2)
    up1, down1 = row_move(feats, 1), row_move(feats, -1)
    up4, down4 = row_move(up2[: rows_dev // 2], 2), row_move(down2[rows_dev // 2 :], -2)
    up3, down3 = row_move(up2, 1), row_move(down2, -1)
    blocks = [feats, down1, down2, down3, up4, up3, up2, up1, down4]
    blocks = [block.reshape(-1, T, T) for block in blocks]

    parts = forward(count, slab_place, col_block, tiles, blocks)
    both = [None] * 4
    for k in (2, 1, 3, 0):
        both[k] = parts[4 + k].astype(F32) + other_core(parts[k]).astype(F32)
    got = [axis_move(both[k].astype(BF), 0, k) for k in (2, 1, 3)]
    total = wide_sum([both[0]] + got)
    parts = [total[0:4]] + [axis_move(total[4 * k : 4 * k + 4].astype(BF), 1, k) for k in (1, 2, 3)]
    parts = [part.reshape(rows_dev, T) for part in parts]

    core = my_c.reshape(1)
    out, base, dzn, keep, give = layer(core, parts, feats, w_self, w_neigh, bias.reshape(1, -1), cotangent)

    half = (keep.astype(F32) + other_core(give).astype(F32)).astype(BF)
    pay = jnp.concatenate([dzn, half], axis=0)
    got = [pay, None, None, None]
    for k in (2, 1, 3):
        got[k] = axis_move(pay, 0, k)
    gw = wide_sum([v[rows_dev:] for v in got]).astype(BF)
    bundle = jnp.concatenate([v[:rows_dev] for v in got] + [gw], axis=0)
    own = [bundle, None, None, None]
    for k in (2, 1, 3):
        own[k] = axis_move(bundle, 1, k)
    far = [other_core(v) for v in own]
    gw = wide_sum([v[4 * rows_dev :] for v in own]).astype(BF)
    swapped = [row_swap(gw, bits) for bits in (1, 4, 5)]

    p = backward(count, section_place, slab_source, tiles, own + far)
    gw, swapped, p = lax.optimization_barrier((gw, swapped, p))
    gw = wide_sum([gw] + swapped).astype(BF)
    up3, down3 = row_move(p[3], 1), row_move(p[5], -1)
    up4, down4 = row_move(p[4], 2), row_move(p[8], -2)
    swapped = row_swap(gw, 2)
    zeros = jnp.zeros((2, T, T), F32)
    up2 = p[2].astype(F32) + up3.astype(F32) + jnp.concatenate([up4.astype(F32), zeros], axis=0)
    down2 = p[6].astype(F32) + down3.astype(F32) + jnp.concatenate([zeros, down4.astype(F32)], axis=0)
    up2, down2 = row_move(up2.astype(BF), 2), row_move(down2.astype(BF), -2)
    up1, down1 = row_move(p[1], 1), row_move(p[7], -1)
    gw = gw.astype(F32) + swapped.astype(F32)
    scale = (1.0 / jnp.sqrt(jnp.float32(total_nodes))).reshape(1)
    grad_feats, grad_self, grad_neigh, grad_bias = finish(
        core, scale, base, p[0], up1, down1, up2, down2, gw, other_core(gw)
    )
    return out, grad_feats, grad_self, grad_neigh, grad_bias.reshape(-1)


def solution(mesh):
    placed = (
        P(("row", "rep"), None),
        P(),
        P(),
        P(),
        P("row", "rep", None, None, None),
        P("row", "rep", None),
        P("row", "rep", None),
        P("row", "rep"),
        P(("row", "rep"), None),
    )
    return jax.shard_map(
        per_device,
        mesh=mesh,
        in_specs=placed,
        out_specs=(P(("row", "rep"), None), P(("row", "rep"), None), P(), P(), P()),
        check_vma=False,
    )
```

```python
import jax
import jax.numpy as jnp
from jax import lax
from jax.experimental import pallas as pl
from jax.experimental.pallas import tpu as pltpu
from jax.sharding import PartitionSpec as P

T = 128
SLOTS = 256
CHUNK = 8
GROUP = 4
HALF = 2 * T + 16
BF = jnp.bfloat16
F32 = jnp.float32
VMEM_LIMIT = 48 * 1024 * 1024

VM = pl.BlockSpec(memory_space=pltpu.VMEM)
SM = pl.BlockSpec(memory_space=pltpu.SMEM)
HB = pl.BlockSpec(memory_space=pl.ANY)


def shape(rows, cols, dtype):
    return jax.ShapeDtypeStruct((rows, cols), dtype)


def other_core(value):
    return lax.ppermute(value, "rep", [(i, i ^ 1) for i in range(32)])


def axis_move(value, which, k):
    return lax.ppermute(value, "rep", [(i, i ^ (k * (8 if i % 2 == which else 2))) for i in range(32)])


def row_move(value, step):
    return lax.ppermute(value, "row", [(i, (i + step) % 8) for i in range(8)])


def row_swap(value, bit):
    return lax.ppermute(value, "row", [(i, i ^ bit) for i in range(8)])


def tile_copy(tiles, tbuf, sem, i):
    part = pl.ds(pl.multiple_of(i * CHUNK, CHUNK), CHUNK)
    return pltpu.make_async_copy(tiles.at[part], tbuf.at[part], sem.at[i])


def start_tiles(count, tiles, tbuf, sem):
    chunks = (count[0] + CHUNK - 1) // CHUNK

    def start(i, carry):
        tile_copy(tiles, tbuf, sem, i).start()
        return carry

    lax.fori_loop(0, chunks, start, 0)
    return chunks


def zero(acc):
    def clear(i, carry):
        acc[i] = jnp.zeros((T, T), F32)
        return carry

    lax.fori_loop(0, acc.shape[0], clear, 0, unroll=4)


def add_products(chunks, tiles, tbuf, sem, product, place, acc):
    def step(i, carry):
        tile_copy(tiles, tbuf, sem, i).wait()
        for g in range(0, CHUNK, GROUP):
            slots = [i * CHUNK + g + k for k in range(GROUP)]
            prods = [product(t) for t in slots]
            for t, prod in zip(slots, prods):
                q = place[t]
                acc[q] = acc[q] + prod
        return carry

    lax.fori_loop(0, chunks, step, 0)


def forward_kernel(count, place, source, tiles, *rest):
    feats, outs = rest[:9], rest[9:17]
    tbuf, fbuf, acc, stage, tsem, fsem, osem = rest[17:]
    loads = []
    for d in range(8):
        if d == 4:
            loads.append(pltpu.make_async_copy(feats[4], fbuf.at[pl.ds(16, 2)], fsem.at[4]))
            loads.append(pltpu.make_async_copy(feats[8], fbuf.at[pl.ds(18, 2)], fsem.at[8]))
        else:
            loads.append(pltpu.make_async_copy(feats[d], fbuf.at[pl.ds(4 * d, 4)], fsem.at[d]))
    for load in loads:
        load.start()
    chunks = start_tiles(count, tiles, tbuf, tsem)
    zero(acc)
    for load in loads:
        load.wait()

    def product(t):
        return jnp.dot(tbuf[t], fbuf[source[t]], preferred_element_type=F32)

    add_products(chunks, tiles, tbuf, tsem, product, place, acc)
    stores = []
    for k in range(8):
        part = pl.ds(16 * k, 16)
        stage[part] = acc[part].astype(BF)
        stores.append(pltpu.make_async_copy(stage.at[part], outs[k], osem.at[k]))
        stores[-1].start()
    for store in stores:
        store.wait()


def forward(count, place, source, tiles, feats):
    blocks = [jax.ShapeDtypeStruct((16, T, T), BF)] * 8
    return pl.pallas_call(
        forward_kernel,
        out_shape=blocks,
        in_specs=[SM, SM, SM, HB] + [HB] * 9,
        out_specs=[HB] * 8,
        scratch_shapes=[
            pltpu.VMEM((SLOTS, T, T), BF),
            pltpu.VMEM((32, T, T), BF),
            pltpu.VMEM((129, T, T), F32),
            pltpu.VMEM((128, T, T), BF),
            pltpu.SemaphoreType.DMA((SLOTS // CHUNK,)),
            pltpu.SemaphoreType.DMA((9,)),
            pltpu.SemaphoreType.DMA((8,)),
        ],
        compiler_params=pltpu.CompilerParams(vmem_limit_bytes=VMEM_LIMIT),
        cost_estimate=pl.CostEstimate(flops=2 * SLOTS * T**3, bytes_accessed=16 * 2**20, transcendentals=0),
        name="tiles_forward",
    )(count, place, source, tiles, *feats)


def backward_kernel(count, place, source, tiles, *rest):
    grads, outs = rest[:8], rest[8:17]
    tbuf, gbuf, acc, stage, tsem, gsem, osem = rest[17:]
    loads = [
        pltpu.make_async_copy(grads[k].at[pl.ds(0, 16 * T)], gbuf.at[pl.ds(16 * T * k, 16 * T)], gsem.at[k])
        for k in range(8)
    ]
    for load in loads:
        load.start()
    chunks = start_tiles(count, tiles, tbuf, tsem)
    zero(acc)
    for load in loads:
        load.wait()

    def product(t):
        grad = gbuf[pl.ds(pl.multiple_of(source[t] * T, T), T)]
        return jnp.dot(grad, tbuf[t], preferred_element_type=F32)

    add_products(chunks, tiles, tbuf, tsem, product, place, acc)
    stores = [pltpu.make_async_copy(acc.at[pl.ds(0, 4)], outs[0], osem.at[0])]
    stores[0].start()
    for d in range(1, 8):
        stage[pl.ds(4 * d, 4)] = acc[pl.ds(4 * d, 4)].astype(BF)
        if d == 4:
            stores.append(pltpu.make_async_copy(stage.at[pl.ds(16, 2)], outs[4], osem.at[4]))
            stores.append(pltpu.make_async_copy(stage.at[pl.ds(18, 2)], outs[8], osem.at[8]))
            stores[-2].start()
        else:
            stores.append(pltpu.make_async_copy(stage.at[pl.ds(4 * d, 4)], outs[d], osem.at[d]))
        stores[-1].start()
    for store in stores:
        store.wait()


def backward(count, place, source, tiles, grads):
    four = jax.ShapeDtypeStruct((4, T, T), BF)
    two = jax.ShapeDtypeStruct((2, T, T), BF)
    outs = [jax.ShapeDtypeStruct((4, T, T), F32), four, four, four, two, four, four, four, two]
    return pl.pallas_call(
        backward_kernel,
        out_shape=outs,
        in_specs=[SM, SM, SM, HB] + [HB] * 8,
        out_specs=[HB] * 9,
        scratch_shapes=[
            pltpu.VMEM((SLOTS, T, T), BF),
            pltpu.VMEM((128 * T, T), BF),
            pltpu.VMEM((33, T, T), F32),
            pltpu.VMEM((32, T, T), BF),
            pltpu.SemaphoreType.DMA((SLOTS // CHUNK,)),
            pltpu.SemaphoreType.DMA((8,)),
            pltpu.SemaphoreType.DMA((9,)),
        ],
        compiler_params=pltpu.CompilerParams(vmem_limit_bytes=VMEM_LIMIT),
        cost_estimate=pl.CostEstimate(flops=2 * SLOTS * T**3, bytes_accessed=16 * 2**20, transcendentals=0),
        name="tiles_backward",
    )(count, place, source, tiles, *grads)


def layer_kernel(core, a0, a1, a2, a3, feats, w_self, w_neigh, bias, cot, out, base, dzn, keep, give, halves):
    agg = (a0[...] + a1[...].astype(F32)) + (a2[...].astype(F32) + a3[...].astype(F32))
    agg = agg.astype(BF)
    x = feats[...]
    z = (
        jnp.dot(x, w_self[...], preferred_element_type=F32)
        + jnp.dot(agg, w_neigh[...], preferred_element_type=F32)
        + bias[...]
    )
    root = 0.7978845608028654
    t = jnp.tanh(root * (z + 0.044715 * (z * z * z)))
    cdf = 0.5 * (1.0 + t)
    out[...] = (z * cdf).astype(BF)
    slope = cdf + 0.5 * z * (1.0 - t * t) * (root * (1.0 + 3.0 * 0.044715 * (z * z)))
    dz = (cot[...].astype(F32) * slope).astype(BF)
    turned = lax.dot_general(w_neigh[...], dz, (((1,), (1,)), ((), ())), preferred_element_type=F32).astype(BF)
    for s in range(4):
        dzn[T * s : T * s + T] = turned[:, T * s : T * s + T]
    both = jnp.concatenate([x, agg], axis=1)
    grads = lax.dot_general(both, dz, (((0,), (0,)), ((), ())), preferred_element_type=F32).astype(BF)
    column = jnp.sum(dz.astype(F32), axis=0, keepdims=True)
    columns = jnp.concatenate([column[:, 0:T], column[:, T : 2 * T]], axis=0)
    high = columns.astype(BF).astype(F32)
    tail = jnp.concatenate([high, columns - high, jnp.zeros((12, T), F32)], axis=0).astype(BF)
    for m in range(2):
        halves[m, 0:T] = grads[T * m : T * m + T, 0:T]
        halves[m, T : 2 * T] = grads[T * m : T * m + T, T : 2 * T]
        halves[m, 2 * T : HALF] = tail
    keep[...] = halves[core[0]]
    give[...] = halves[1 - core[0]]
    base[...] = lax.dot_general(dz, w_self[...], (((1,), (1,)), ((), ())), preferred_element_type=F32)


def layer(core, parts, feats, w_self, w_neigh, bias, cot):
    rows = feats.shape[0]
    half = shape(HALF, T, BF)
    return pl.pallas_call(
        layer_kernel,
        out_shape=[shape(rows, 2 * T, BF), shape(rows, T, F32), shape(rows, T, BF), half, half],
        in_specs=[SM] + [VM] * 9,
        out_specs=[VM] * 5,
        scratch_shapes=[pltpu.VMEM((2, HALF, T), BF)],
        compiler_params=pltpu.CompilerParams(vmem_limit_bytes=VMEM_LIMIT),
        name="layer",
    )(core, *parts, feats, w_self, w_neigh, bias, cot)


def finish_kernel(core, scale, base, p0, f1, b1, f2, b2, mine, theirs, grad, g_self, g_neigh, g_bias):
    for s in range(4):
        spread = (
            p0[s] + (f1[s].astype(F32) + b1[s].astype(F32)) + (f2[s].astype(F32) + b2[s].astype(F32))
        )
        grad[T * s : T * s + T] = base[T * s : T * s + T] + spread.T
    first = core[0] == 0
    own, other = mine[...] * scale[0], theirs[...] * scale[0]
    low, high = jnp.where(first, own, other), jnp.where(first, other, own)
    for g, part in ((g_self, low), (g_neigh, high)):
        g[:, 0:T] = part[0:T]
        g[:, T : 2 * T] = part[T : 2 * T]
    g_bias[...] = low[2 * T : 2 * T + 2] + low[2 * T + 2 : 2 * T + 4]


def finish(core, scale, base, p0, f1, b1, f2, b2, mine, theirs):
    return pl.pallas_call(
        finish_kernel,
        out_shape=[
            shape(base.shape[0], T, F32), shape(T, 2 * T, F32), shape(T, 2 * T, F32), shape(2, T, F32)
        ],
        in_specs=[SM, SM] + [VM] * 8,
        out_specs=[VM] * 4,
        name="finish",
    )(core, scale, base, p0, f1, b1, f2, b2, mine, theirs)


def wide_sum(values):
    values = [value.astype(F32) for value in values]
    return (values[0] + values[1]) + (values[2] + values[3])


def per_device(feats, w_self, w_neigh, bias, tiles, tile_row, tile_col, tile_count, cotangent):
    rows_dev, width = feats.shape
    total_nodes = rows_dev * 256
    tiles = tiles.reshape(SLOTS, T, T)
    my_z = lax.axis_index("row")
    my_rep = lax.axis_index("rep")
    my_x, my_y, my_c = my_rep // 8, (my_rep // 2) % 4, my_rep % 2
    count = tile_count.reshape(1)
    live = jnp.arange(SLOTS, dtype=jnp.int32) < count
    row = tile_row.reshape(SLOTS)
    col = tile_col.reshape(SLOTS)

    owner, sub = row // 4, row % 4
    kx, ky, kc = (owner // 8) ^ my_x, ((owner // 2) % 4) ^ my_y, (owner % 2) ^ my_c
    k1, k2 = jnp.where(owner % 2 == 0, kx, ky), jnp.where(owner % 2 == 0, ky, kx)
    slab_place = jnp.where(live, 64 * (1 - kc) + (k1 * 4 + k2) * 4 + sub, 128)
    slab_source = 64 * kc + (k2 * 4 + k1) * 4 + sub
    col_block = ((col // 4 - my_z) % 8) * 4 + col % 4
    section_place = jnp.where(live, col_block, 32)

    up2, down2 = row_move(feats, 2), row_move(feats, -2)
    up1, down1 = row_move(feats, 1), row_move(feats, -1)
    up4, down4 = row_move(up2[: rows_dev // 2], 2), row_move(down2[rows_dev // 2 :], -2)
    up3, down3 = row_move(up2, 1), row_move(down2, -1)
    blocks = [feats, down1, down2, down3, up4, up3, up2, up1, down4]
    blocks = [block.reshape(-1, T, T) for block in blocks]

    parts = forward(count, slab_place, col_block, tiles, blocks)
    both = [None] * 4
    for k in (2, 1, 3, 0):
        both[k] = parts[4 + k].astype(F32) + other_core(parts[k]).astype(F32)
    got = [axis_move(both[k].astype(BF), 0, k) for k in (2, 1, 3)]
    total = wide_sum([both[0]] + got)
    parts = [total[0:4]] + [axis_move(total[4 * k : 4 * k + 4].astype(BF), 1, k) for k in (1, 2, 3)]
    parts = [part.reshape(rows_dev, T) for part in parts]

    core = my_c.reshape(1)
    out, base, dzn, keep, give = layer(core, parts, feats, w_self, w_neigh, bias.reshape(1, -1), cotangent)

    half = (keep.astype(F32) + other_core(give).astype(F32)).astype(BF)
    pay = jnp.concatenate([dzn, half], axis=0)
    got = [pay, None, None, None]
    for k in (2, 1, 3):
        got[k] = axis_move(pay, 0, k)
    gw = wide_sum([v[rows_dev:] for v in got]).astype(BF)
    bundle = jnp.concatenate([v[:rows_dev] for v in got] + [gw], axis=0)
    own = [bundle, None, None, None]
    for k in (2, 1, 3):
        own[k] = axis_move(bundle, 1, k)
    far = [other_core(v) for v in own]
    gw = wide_sum([v[4 * rows_dev :] for v in own]).astype(BF)
    swapped = [row_swap(gw, bits) for bits in (2, 4, 6)]

    p = backward(count, section_place, slab_source, tiles, own + far)
    gw, swapped, p = lax.optimization_barrier((gw, swapped, p))
    gw = wide_sum([gw] + swapped).astype(BF)
    up3, down3 = row_move(p[3], 1), row_move(p[5], -1)
    up4, down4 = row_move(p[4], 2), row_move(p[8], -2)
    swapped = row_swap(gw, 1)
    zeros = jnp.zeros((2, T, T), F32)
    up2 = p[2].astype(F32) + up3.astype(F32) + jnp.concatenate([up4.astype(F32), zeros], axis=0)
    down2 = p[6].astype(F32) + down3.astype(F32) + jnp.concatenate([zeros, down4.astype(F32)], axis=0)
    up2, down2 = row_move(up2.astype(BF), 2), row_move(down2.astype(BF), -2)
    up1, down1 = row_move(p[1], 1), row_move(p[7], -1)
    gw = gw.astype(F32) + swapped.astype(F32)
    scale = (1.0 / jnp.sqrt(jnp.float32(total_nodes))).reshape(1)
    grad_feats, grad_self, grad_neigh, grad_bias = finish(
        core, scale, base, p[0], up1, down1, up2, down2, gw, other_core(gw)
    )
    return out, grad_feats, grad_self, grad_neigh, grad_bias.reshape(-1)


def solution(mesh):
    placed = (
        P(("row", "rep"), None),
        P(),
        P(),
        P(),
        P("row", "rep", None, None, None),
        P("row", "rep", None),
        P("row", "rep", None),
        P("row", "rep"),
        P(("row", "rep"), None),
    )
    return jax.shard_map(
        per_device,
        mesh=mesh,
        in_specs=placed,
        out_specs=(P(("row", "rep"), None), P(("row", "rep"), None), P(), P(), P()),
        check_vma=False,
    )
```
